128 devices in a mesh: member: 16 (over z, x_lo, core), fsdp: 8 (over x_hi, y).
Axes of the slice: x: 4 (x_hi: 2, x_lo: 2; x = x_hi * 2 + x_lo), y: 4, z: 4, core: 2. Of those that a mesh axis runs over, the one named last changes fastest.
Arguments:
- hidden: bfloat16 [16, 3072, 3584], P('member', 'fsdp'), may hold values from -6 to 6
- value_grad: bfloat16 [16, 3072, 2048], P('member', 'fsdp'), may hold values from -1.796875 to 1.796875
- weight: bfloat16 [16, 3584, 2048], P('member', 'fsdp'), may hold values from -0.09375 to 0.09375
- moment_one: bfloat16 [16, 3584, 2048], P('member', 'fsdp'), may hold values from -6 to 6
- moment_two: bfloat16 [16, 3584, 2048], P('member', 'fsdp'), may hold values from 0.5 to 8
- norm_gain: float32 [16, 3584], P('member'), may hold values from -0.5 to 0.5
- gain_first: float32 [16, 3584], P('member'), may hold values from -6 to 6
- gain_second: float32 [16, 3584], P('member'), may hold values from 0.3 to 10
- donors: int32 [16], replicated, may hold values from 0 to 15
- recipient: int32 [16], replicated, may hold values 0 or 1
Outputs:
- values: bfloat16 [16, 3072, 2048], P('member', 'fsdp')
- hidden_grad: bfloat16 [16, 3072, 3584], P('member', 'fsdp')
- weight_out: bfloat16 [16, 3584, 2048], P('member', 'fsdp')
- first_out: bfloat16 [16, 3584, 2048], P('member', 'fsdp')
- second_out: bfloat16 [16, 3584, 2048], P('member', 'fsdp')
- gain_out: float32 [16, 3584], P('member')
- gain_first_out: float32 [16, 3584], P('member')
- gain_second_out: float32 [16, 3584], P('member')
The draws below stay inside these ranges and needn't reach their ends.
All inputs are finite; a program needn't handle non-finite values.
Results may differ from the reference program's by a relative error of at most 0.015.
Values may be sent and summed in bfloat16 or wider, within the bound.
No kernel may reach another device: no remote copies, remote signals or barrier semaphores. Data moves between devices by JAX's collectives and lax.ppermute only.
A program may use at most 192 MiB of HBM per device.

```python
import math
import jax
import jax.numpy as jnp
from jax import lax

D = 3584
KV = 2048
TOK_DEV = 384
STEP = 100
MEMBERS = 16
TOKENS = 3072
N_FSDP = 8


def set_ends(result, own_key, low, high):
    shape = result.shape
    place = [jax.random.randint(jax.random.fold_in(own_key, axis), (), 0, shape[axis]) for axis in range(len(shape))]
    result = result.at[tuple(place)].set(low)
    longest = shape.index(max(shape))
    place[longest] = (place[longest] + 1) % shape[longest]
    return result.at[tuple(place)].set(high)


def level_of(key, dims, cuts, least, high):
    factor_of, own = 1.0, jax.random.fold_in(key, 6)
    for position, parts in cuts:
        draws = jnp.exp(jax.random.uniform(jax.random.fold_in(own, position), (parts,), jnp.float32, least / len(cuts), high / len(cuts)))
        factor_of = factor_of * jnp.repeat(draws, dims[position] // parts).reshape([-1 if axis == position else 1 for axis in range(len(dims))])
    return factor_of


def centred(stream_key, dims, scale, reach, pieces=(), kind=jnp.bfloat16):
    array = scale * jax.random.normal(stream_key, dims, jnp.float32)
    if pieces:
        array = array * level_of(stream_key, dims, pieces, -0.22, 0.18)
    return jnp.clip(array, -reach, reach).astype(kind)


def setup_inputs(seed: int = 0) -> dict:
    key_list = jax.random.split(jax.random.key(seed), 11)
    return {
        "hidden": centred(key_list[0], (MEMBERS, TOKENS, D), 1.0, 6.0, ((0, 16), (1, 8))),
        "value_grad": centred(key_list[1], (MEMBERS, TOKENS, KV), 0.3, 1.796875, ((0, 16), (1, 8))),
        "weight": centred(key_list[2], (MEMBERS, D, KV), D ** -0.5, 0.09375, ((0, 16), (1, 8))),
        "moment_one": centred(key_list[3], (MEMBERS, D, KV), 1.0, 6.0, ((0, 16), (1, 8))),
        "moment_two": jnp.clip(jnp.exp(math.log(8.0) - 2.7725887 * jax.random.uniform(key_list[4], (MEMBERS, D, KV), jnp.float32) ** level_of(key_list[4], (MEMBERS, D, KV), ((0, 16), (1, 8)), -0.2, 0.2)), 0.5, 8.0).astype(jnp.bfloat16),
        "norm_gain": jnp.clip(jax.random.uniform(key_list[5], (MEMBERS, D), jnp.float32, -0.5, 0.5) * level_of(key_list[5], (MEMBERS, D), ((0, 16),), -0.4, 0.0), -0.5, 0.5),
        "gain_first": centred(key_list[6], (MEMBERS, D), 1.0, 6.0, ((0, 16),), jnp.float32),
        "gain_second": jnp.clip(jnp.exp(math.log(10.0) - 3.506558 * jax.random.uniform(key_list[7], (MEMBERS, D), jnp.float32) ** level_of(key_list[7], (MEMBERS, D), ((0, 16),), -0.2, 0.2)), 0.3, 10.0),
        "donors": set_ends(jax.random.randint(key_list[8], (MEMBERS,), 0, MEMBERS), jax.random.fold_in(key_list[8], 1), 0, MEMBERS - 1).astype(jnp.int32),
        "recipient": set_ends((jax.random.randint(key_list[9], (MEMBERS,), 0, 2) < 1).astype(jnp.int32), jax.random.fold_in(key_list[9], 1), 0, 1),
    }


beta_one = 0.9
beta_two = 0.999
adam_eps = 1e-08
learn_rate = 0.001
decay_rate = 0.1
norm_eps = 1e-06

def adam_update(param, grad, first, second, decay):
    first_new = beta_one * first + (1.0 - beta_one) * grad
    second_new = beta_two * second + (1.0 - beta_two) * grad * grad
    corr_one = 1.0 - beta_one ** STEP
    corr_two = 1.0 - beta_two ** STEP
    step_dir = first_new / corr_one / (jnp.sqrt(second_new / corr_two) + adam_eps) + decay * param
    return (param - learn_rate * step_dir, first_new, second_new)

def one_member(items):
    hidden, value_grad, weight, moment_one, moment_two, norm_gain, gain_first, gain_second = items
    wide = hidden.astype(jnp.float32)
    scale = lax.rsqrt(lax.optimization_barrier(jnp.mean(wide * wide, axis=-1, keepdims=True)) + norm_eps)
    normed = wide * scale
    factor = 1.0 + norm_gain
    inputs = (normed * factor).astype(jnp.bfloat16)
    values = jnp.dot(inputs, weight, preferred_element_type=jnp.float32).astype(jnp.bfloat16)
    input_grad = jnp.dot(value_grad, weight.T, preferred_element_type=jnp.float32)
    gain_grad = lax.optimization_barrier(jnp.sum(input_grad * normed, axis=0))
    scaled = input_grad * factor
    hidden_grad = (scale * (scaled - normed * lax.optimization_barrier(jnp.mean(scaled * normed, axis=-1, keepdims=True)))).astype(jnp.bfloat16)
    blocks_in = inputs.reshape(N_FSDP, TOK_DEV, D)
    blocks_grad = value_grad.reshape(N_FSDP, TOK_DEV, KV)

    def add_block(total, index):
        part = jnp.dot(blocks_in[index].T, blocks_grad[index], preferred_element_type=jnp.float32)
        part = lax.optimization_barrier(part.astype(jnp.bfloat16))
        return (total + part.astype(jnp.float32), None)
    weight_grad, _ = lax.scan(add_block, jnp.zeros((D, KV), jnp.float32), jnp.arange(N_FSDP, dtype=jnp.int32))
    updated, first, second = adam_update(weight.astype(jnp.float32), weight_grad, moment_one.astype(jnp.float32), moment_two.astype(jnp.float32), decay_rate)
    new_gain, new_first, new_second = adam_update(norm_gain, gain_grad, gain_first, gain_second, 0.0)
    return (values, hidden_grad, updated.astype(jnp.bfloat16), first.astype(jnp.bfloat16), second.astype(jnp.bfloat16), new_gain, new_first, new_second)

def reference(hidden, value_grad, weight, moment_one, moment_two, norm_gain, gain_first, gain_second, donors, recipient):
    outs = lax.map(one_member, (hidden, value_grad, weight, moment_one, moment_two, norm_gain, gain_first, gain_second))
    source = jnp.where(recipient == 1, donors, jnp.arange(MEMBERS, dtype=jnp.int32)).astype(jnp.int32)
    values, hidden_grad = (outs[0], outs[1])
    rest = [jnp.take(item, source, axis=0) for item in outs[2:]]
    return (values, hidden_grad, rest[0], rest[1], rest[2], rest[3], rest[4], rest[5])
```

```python
import jax
import jax.numpy as jnp
from jax import lax
from jax.sharding import PartitionSpec as P

STEP = 100
beta_one = 0.9
beta_two = 0.999
adam_eps = 1e-08
learn_rate = 0.001
decay_rate = 0.1
norm_eps = 1e-06

BF16 = jnp.bfloat16
F32 = jnp.float32
CHUNKS = 2


def adam_update(param, grad, first, second, decay):
    first_new = beta_one * first + (1.0 - beta_one) * grad
    second_new = beta_two * second + (1.0 - beta_two) * grad * grad
    corr_one = 1.0 - beta_one**STEP
    corr_two = 1.0 - beta_two**STEP
    step_dir = first_new / corr_one / (jnp.sqrt(second_new / corr_two) + adam_eps) + decay * param
    return (param - learn_rate * step_dir, first_new, second_new)


def to_member(x, dz=0, dx=0, dc=0):
    pairs = [
        (m, ((m // 4 + dz) % 4) * 4 + ((m // 2 % 2) ^ dx) * 2 + ((m % 2) ^ dc)) for m in range(16)
    ]
    return lax.ppermute(x, "member", pairs)


def to_fsdp(x, dx=0, dy=0):
    pairs = [(f, ((f // 4) ^ dx) * 4 + (f % 4 + dy) % 4) for f in range(8)]
    return lax.ppermute(x, "fsdp", pairs)


Y_GROUPS = [[0, 1, 2, 3], [4, 5, 6, 7]]


def pick(x, index, axis=0):
    return lax.dynamic_index_in_dim(x, index, axis, keepdims=False)


def put(x, part, index, axis=0):
    return lax.dynamic_update_index_in_dim(x, part, index, axis)


def matmul(a, b, contract):
    return lax.dot_general(a, b, ((contract[:1], contract[1:]), ((), ())), preferred_element_type=F32)


def crossing(source):
    own = jnp.arange(16, dtype=jnp.int32)
    src = source.reshape(4, 4).T
    group_x = (jnp.arange(4, dtype=jnp.int32) // 2)[:, None]
    cross = (src // 2) % 2 != group_x
    same = src[:, :, None] == src[:, None, :]
    first_same = jnp.argmax(same, axis=2).astype(jnp.int32)
    is_first = cross & (first_same == jnp.arange(4, dtype=jnp.int32)[None, :])
    rank = jnp.cumsum(is_first.astype(jnp.int32), axis=1) - 1
    slot = jnp.sum(
        jnp.where(first_same[:, :, None] == jnp.arange(4)[None, None, :], rank[:, None, :], 0), axis=2
    )
    count = jnp.max(jnp.sum(is_first.astype(jnp.int32), axis=1))
    slots = jnp.arange(4, dtype=jnp.int32)
    holds = is_first[:, :, None] & (rank[:, :, None] == slots[None, None, :])
    slot_src = jnp.sum(jnp.where(holds, src[:, :, None], 0), axis=1)
    return src, cross, slot, slot_src, count


def shards(
    hidden,
    value_grad,
    weight,
    moment_one,
    moment_two,
    norm_gain,
    gain_first,
    gain_second,
    donors,
    recipient,
):
    member = lax.axis_index("member")
    fsdp = lax.axis_index("fsdp")
    z, xl, core = member // 4, (member // 2) % 2, member % 2
    xh, y = fsdp // 4, fsdp % 4
    z_at = [(z + d) % 4 for d in range(4)]
    z_from = [(z - d) % 4 for d in range(4)]
    y_at = [(y + d) % 4 for d in range(4)]
    y_from = [(y - d) % 4 for d in range(4)]

    tokens, features = hidden.shape[1:]
    width = value_grad.shape[2]
    rows = features // 8
    cut = width // CHUNKS
    part = rows // 4

    w_own = weight[0]
    w_other = to_fsdp(w_own, dx=1)

    wide = hidden[0].astype(F32)
    scale = lax.rsqrt(jnp.mean(wide * wide, axis=-1, keepdims=True) + norm_eps)
    normed = wide * scale
    factor = 1.0 + norm_gain[0]
    inputs = (normed * factor).astype(BF16)
    blocks = inputs.reshape(tokens, 8, rows).transpose(1, 0, 2).reshape(2, 4, tokens, rows)
    blocks = jnp.where(xh == 0, blocks, blocks[::-1])
    x_own = jnp.zeros((4, tokens, rows), BF16)
    x_other = jnp.zeros((4, tokens, rows), BF16)
    for d in range(4):
        block = pick(blocks, y_at[d], 1)
        got = to_fsdp(block, dy=d) if d else block
        x_own = put(x_own, got[0], y_from[d])
        x_other = put(x_other, got[1], y_from[d])
    x_own = x_own.reshape(4 * tokens, rows)
    x_other = x_other.reshape(4 * tokens, rows)

    cots = [
        lax.all_gather(
            value_grad[0, :, i * cut : (i + 1) * cut], "fsdp", axis_index_groups=Y_GROUPS, tiled=True
        )
        for i in range(CHUNKS)
    ]

    state = jnp.stack([weight[0], moment_one[0], moment_two[0]]).reshape(3, 4, part, width)
    held = []
    for d in range(4):
        block = pick(state, z_at[d], 1)
        held.append(to_member(block, dz=d) if d else block)

    own_index = jnp.arange(16, dtype=jnp.int32)
    source = jnp.where(recipient == 1, donors, own_index)
    src, cross, slot, slot_src, count = crossing(source)
    group = xl * 2 + core
    group_other = (1 - xl) * 2 + core
    my_src, my_cross, my_slot = pick(src, group), pick(cross, group), pick(slot, group)
    send_src = pick(slot_src, group_other)

    returned = []
    for i in range(CHUNKS):
        cot = cots[i]
        to_send = matmul(x_other, cot, (0, 0)).astype(BF16)
        arrived = to_fsdp(to_send, dx=1)
        grad = (matmul(x_own, cot, (0, 0)) + arrived.astype(F32)).astype(BF16)
        grad = grad.reshape(4, part, cut)
        mine = []
        for d in range(4):
            block = pick(grad, z_at[d])
            got = to_member(block, dz=d) if d else block
            here = held[d][:, :, i * cut : (i + 1) * cut].astype(F32)
            new = adam_update(here[0], got.astype(F32), here[1], here[2], decay_rate)
            mine.append(jnp.stack(new).astype(BF16))
        mine = jnp.stack(mine)
        theirs = to_member(mine, dc=1)

        def local(s):
            place = (z - s // 4) % 4
            return jnp.where(s % 2 == core, pick(mine, place), pick(theirs, place))

        def branch(n):
            def run(_):
                if n == 0:
                    return jnp.zeros_like(mine)
                sent = jnp.stack([local(send_src[j]) for j in range(n)])
                came = to_member(sent, dx=1)
                return jnp.concatenate([came, jnp.zeros((4 - n,) + came.shape[1:], BF16)])

            return run

        far = lax.switch(count, [branch(n) for n in range(5)], 0)
        back = []
        for d in range(4):
            s = pick(my_src, z_at[d])
            chosen = jnp.where(pick(my_cross, z_at[d]), pick(far, pick(my_slot, z_at[d])), local(s))
            back.append(to_member(chosen, dz=d) if d else chosen)
        returned.append(back)

    outs = []
    for k in range(3):
        out = jnp.zeros((4, part, width), BF16)
        for i in range(CHUNKS):
            for d in range(4):
                out = lax.dynamic_update_slice(
                    out, returned[i][d][k][None], (z_from[d], jnp.int32(0), jnp.int32(i * cut))
                )
        outs.append(out.reshape(1, rows, width))

    value_part = (matmul(x_own, w_own, (1, 0)) + matmul(x_other, w_other, (1, 0))).astype(BF16)
    values = lax.psum_scatter(value_part, "fsdp", axis_index_groups=Y_GROUPS, tiled=True)

    def input_grad_of(w):
        total = 0.0
        for i in range(CHUNKS):
            total = total + matmul(cots[i], w[:, i * cut : (i + 1) * cut], (1, 1))
        return total

    g_own, g_other = input_grad_of(w_own), input_grad_of(w_other)
    gain_part = jnp.stack(
        [jnp.sum(g_own * x_own.astype(F32), axis=0), jnp.sum(g_other * x_other.astype(F32), axis=0)]
    )
    gain_sum = gain_part + to_fsdp(gain_part, dx=1)[::-1]
    g_pair = jnp.stack([g_own.astype(BF16), g_other.astype(BF16)]).reshape(2, 4, tokens, rows)
    back_own = jnp.zeros((4, tokens, rows), BF16)
    back_other = jnp.zeros((4, tokens, rows), BF16)
    for d in range(4):
        block = pick(g_pair, y_at[d], 1)
        got = to_fsdp(block, dy=d) if d else block
        back_own = put(back_own, got[0], y_from[d])
        back_other = put(back_other, got[1], y_from[d])
    input_grad = jnp.concatenate(
        [jnp.where(xh == 0, back_own, back_other), jnp.where(xh == 0, back_other, back_own)]
    )
    input_grad = input_grad.transpose(1, 0, 2).reshape(tokens, features).astype(F32)
    scaled = input_grad * factor
    hidden_grad = (
        scale * (scaled - normed * jnp.mean(scaled * normed, axis=-1, keepdims=True))
    ).astype(BF16)

    def quarter(v):
        both = pick(v[0].reshape(2, 4, rows), y, 1)
        return jnp.where(xh == 0, both, both[::-1])

    gain_q = quarter(norm_gain)
    gain_grad = gain_sum / (1.0 + gain_q)
    gain_new = jnp.stack(
        adam_update(gain_q, gain_grad, quarter(gain_first), quarter(gain_second), 0.0)
    )
    along_z = jnp.stack([gain_new] + [to_member(gain_new, dz=d) for d in (1, 2, 3)])
    chip = jnp.stack([along_z, to_member(along_z, dc=1)])
    every = jnp.stack([chip, to_member(chip, dx=1)])
    s = pick(source, member)
    chosen = every[(s // 2 % 2) ^ xl, (s % 2) ^ core, (z - s // 4) % 4]
    gain_all = jnp.zeros((3, 2, 4, rows), F32)
    for d in range(4):
        got = to_fsdp(chosen, dy=d) if d else chosen
        gain_all = put(gain_all, got, y_from[d], 2)
    gain_all = jnp.where(xh == 0, gain_all, gain_all[:, ::-1]).reshape(3, 1, features)
    return (values[None], hidden_grad[None], *outs, gain_all[0], gain_all[1], gain_all[2])


def solution(mesh):
    tok = P("member", "fsdp", None)
    mem = P("member", None)
    return jax.shard_map(
        shards,
        mesh=mesh,
        in_specs=(tok,) * 5 + (mem,) * 3 + (P(), P()),
        out_specs=(tok,) * 5 + (mem,) * 3,
        check_vma=False,
    )
```

```python
import functools

import jax
import jax.numpy as jnp
from jax import lax
from jax.experimental import pallas as pl
from jax.experimental.pallas import tpu as pltpu
from jax.sharding import PartitionSpec as P

STEP = 100
beta_one = 0.9
beta_two = 0.999
adam_eps = 1e-08
learn_rate = 0.001
decay_rate = 0.1
norm_eps = 1e-06

BF16 = jnp.bfloat16
F32 = jnp.float32
CHUNKS = 2
SLOTS = 3

Y_GROUPS = [[0, 1, 2, 3], [4, 5, 6, 7]]
X_GROUPS = [[p // 2 * 4 + x * 2 + p % 2 for p in range(8)] for x in range(2)]
PARAMS = pltpu.CompilerParams(vmem_limit_bytes=56 * 1024 * 1024)
STORE_PARAMS = pltpu.CompilerParams(vmem_limit_bytes=16 * 1024 * 1024)


def adam_update(param, grad, first, second, decay):
    first_new = beta_one * first + (1.0 - beta_one) * grad
    second_new = beta_two * second + (1.0 - beta_two) * grad * grad
    corr_one = 1.0 - beta_one**STEP
    corr_two = 1.0 - beta_two**STEP
    step_dir = first_new / corr_one / (jnp.sqrt(second_new / corr_two) + adam_eps) + decay * param
    return (param - learn_rate * step_dir, first_new, second_new)


def to_fsdp(x, dx=0, dy=0):
    pairs = [(f, ((f // 4) ^ dx) * 4 + (f % 4 + dy) % 4) for f in range(8)]
    return lax.ppermute(x, "fsdp", pairs)


def to_member(x, dz=0, dx=0, dc=0):
    pairs = [
        (m, ((m // 4 + dz) % 4) * 4 + ((m // 2 % 2) ^ dx) * 2 + ((m % 2) ^ dc)) for m in range(16)
    ]
    return lax.ppermute(x, "member", pairs)


def swap_members(x):
    return lax.all_to_all(x, "member", 0, 0, axis_index_groups=X_GROUPS)


def pick(x, index, axis=0):
    return lax.dynamic_index_in_dim(x, index, axis, keepdims=False)


def tie(x, *others):
    return lax.optimization_barrier((x, others))[0]


def put(x, part, index, axis=0):
    return lax.dynamic_update_index_in_dim(x, part, index, axis)


def matmul(a, b, contract):
    return lax.dot_general(a, b, ((contract[:1], contract[1:]), ((), ())), preferred_element_type=F32)


SMALL = pl.CostEstimate(flops=0, bytes_accessed=65536, transcendentals=0)
LARGE = pl.CostEstimate(flops=20_000_000_000, bytes_accessed=10_000_000, transcendentals=0)
ANYWHERE = pl.BlockSpec(memory_space=pl.ANY)


def split_kernel(xh_ref, hidden_ref, gain_ref, out_ref):
    wide = hidden_ref[...].astype(F32)
    scale = lax.rsqrt(jnp.mean(wide * wide, axis=-1, keepdims=True) + norm_eps)
    full = wide * scale * (1.0 + gain_ref[...])
    half = full.shape[1] // 2
    rows = half // 4
    low, high = full[:, :half], full[:, half:]
    swap = xh_ref[0] == 1
    first, second = jnp.where(swap, high, low), jnp.where(swap, low, high)
    for q in range(4):
        part = slice(q * rows, (q + 1) * rows)
        out_ref[q] = jnp.concatenate([first[:, part], second[:, part]], axis=1).astype(BF16)


def split_inputs(hidden, gain, xh):
    tokens, features = hidden.shape
    step = 96
    return pl.pallas_call(
        split_kernel,
        grid_spec=pltpu.PrefetchScalarGridSpec(
            num_scalar_prefetch=1,
            grid=(tokens // step,),
            in_specs=[
                pl.BlockSpec((step, features), lambda i, s: (i, 0)),
                pl.BlockSpec((1, features), lambda i, s: (0, 0)),
            ],
            out_specs=pl.BlockSpec((4, step, features // 4), lambda i, s: (0, i, 0)),
        ),
        out_shape=jax.ShapeDtypeStruct((4, tokens, features // 4), BF16),
        compiler_params=PARAMS,
        cost_estimate=SMALL,
        name="split_inputs",
    )(xh[None], hidden, gain)


def join_kernel(place_ref, hidden_ref, gain_ref, *refs):
    ins, value_refs, (out_ref, values_ref) = refs[:4], refs[4:9], refs[9:]
    xh, y = place_ref[0], place_ref[1]
    total = value_refs[0][...].astype(F32)
    for ref in value_refs[1:3]:
        total = total + ref[...].astype(F32)
    half = total.shape[1] // 2
    for k, ref in enumerate(value_refs[3:]):
        at = slice(k * half, (k + 1) * half)
        values_ref[:, at] = (total[:, at] + ref[...].astype(F32)).astype(BF16)
    wide = hidden_ref[...].astype(F32)
    scale = lax.rsqrt(jnp.mean(wide * wide, axis=-1, keepdims=True) + norm_eps)
    normed = wide * scale
    rows = ins[0].shape[1] // 2
    came = [ref[...].astype(F32) for ref in ins]
    parts = []
    for q in range(4):
        d = lax.rem(y + (4 - q), 4)
        part = came[0]
        for k in (1, 2, 3):
            part = jnp.where(d == k, came[k], part)
        parts.append(part)
    first = jnp.concatenate([p[:, :rows] for p in parts], axis=1)
    second = jnp.concatenate([p[:, rows:] for p in parts], axis=1)
    swap = xh == 1
    grad = jnp.concatenate([jnp.where(swap, second, first), jnp.where(swap, first, second)], axis=1)
    scaled = grad * (1.0 + gain_ref[...])
    mean = jnp.mean(scaled * normed, axis=-1, keepdims=True)
    out_ref[...] = (scale * (scaled - normed * mean)).astype(BF16)


def join_parts(hidden, gain, parts, values, xh, y):
    tokens, features = hidden.shape
    step = 96
    row = lambda i, s: (i, 0)
    return pl.pallas_call(
        join_kernel,
        grid_spec=pltpu.PrefetchScalarGridSpec(
            num_scalar_prefetch=1,
            grid=(tokens // step,),
            in_specs=[
                pl.BlockSpec((step, features), row),
                pl.BlockSpec((1, features), lambda i, s: (0, 0)),
            ]
            + [pl.BlockSpec((step, features // 4), row)] * 4
            + [pl.BlockSpec((step, value.shape[1]), row) for value in values],
            out_specs=[
                pl.BlockSpec((step, features), row),
                pl.BlockSpec((step, values[0].shape[1]), row),
            ],
        ),
        out_shape=[
            jax.ShapeDtypeStruct((tokens, features), BF16),
            jax.ShapeDtypeStruct(values[0].shape, BF16),
        ],
        compiler_params=PARAMS,
        cost_estimate=LARGE,
        name="join_parts",
    )(jnp.stack([xh, y]), hidden, gain, *parts, *values)


def spread_kernel(*refs):
    ins, outs = refs[:3], refs[3:]
    cc = outs[0].shape[3]
    for i, out_ref in enumerate(outs):
        for g in range(2):
            at = (2 * i + g) * cc
            for k in range(3):
                out_ref[g, k] = ins[k][:, at : at + cc]


def spread_states(arrays):
    rows, width = arrays[0].shape
    part, cc = rows // 4, width // CHUNKS // 2
    return pl.pallas_call(
        spread_kernel,
        grid=(4,),
        in_specs=[pl.BlockSpec((part, width), lambda q: (q, 0))] * 3,
        out_specs=[pl.BlockSpec((2, 3, part, cc), lambda q: (q, 0, 0, 0))] * CHUNKS,
        out_shape=[jax.ShapeDtypeStruct((8, 3, part, cc), BF16)] * CHUNKS,
        compiler_params=PARAMS,
        cost_estimate=SMALL,
        name="spread_states",
    )(*arrays)


def add_kernel(here_ref, came_ref, out_ref):
    cc = out_ref.shape[2]
    for g in range(2):
        at = slice(g * cc, (g + 1) * cc)
        out_ref[g] = (here_ref[:, at].astype(F32) + came_ref[:, at].astype(F32)).astype(BF16)


def add_halves(here, came):
    rows, cut = came.shape
    part = rows // 4
    return pl.pallas_call(
        add_kernel,
        grid=(4,),
        in_specs=[pl.BlockSpec((part, cut), lambda q: (q, 0))] * 2,
        out_specs=pl.BlockSpec((2, part, cut // 2), lambda q: (q, 0, 0)),
        out_shape=jax.ShapeDtypeStruct((8, part, cut // 2), BF16),
        compiler_params=PARAMS,
        cost_estimate=SMALL,
        name="add_halves",
    )(here, came)


def take_pieces(pool, places):
    number, block = places.shape[0], pool.shape[1:]

    def kernel(places_ref, pool_ref, out_ref, buffers, sems):
        loads = [
            pltpu.make_async_copy(pool_ref.at[places_ref[j]], buffers.at[j], sems.at[0, j])
            for j in range(number)
        ]
        stores = [
            pltpu.make_async_copy(buffers.at[j], out_ref.at[j], sems.at[1, j]) for j in range(number)
        ]
        for load in loads:
            load.start()
        for load, back in zip(loads, stores):
            load.wait()
            back.start()
        for back in stores:
            back.wait()

    return pl.pallas_call(
        kernel,
        in_specs=[pl.BlockSpec(memory_space=pltpu.SMEM), ANYWHERE],
        out_specs=ANYWHERE,
        out_shape=jax.ShapeDtypeStruct((number,) + block, BF16),
        scratch_shapes=[pltpu.VMEM((number,) + block, BF16), pltpu.SemaphoreType.DMA((2, number))],
        compiler_params=PARAMS,
        cost_estimate=SMALL,
        name="take_pieces",
    )(places, pool)


def adam_kernel(table_ref, *refs):
    pools, out_ref = refs[:4], refs[4]
    step = 16

    def run(held_ref, grad_ref):
        for i in range(grad_ref.shape[1] // step):
            at = slice(i * step, (i + 1) * step)
            state = [held_ref[0, k, at, :].astype(F32) for k in range(3)]
            grad = grad_ref[0, at, :].astype(F32)
            new = adam_update(state[0], grad, state[1], state[2], decay_rate)
            for k in range(3):
                out_ref[0, k, at, :] = new[k].astype(BF16)

    far = table_ref[0, pl.program_id(0)]

    @pl.when(far == 0)
    def _():
        run(pools[0], pools[1])

    @pl.when(far == 1)
    def _():
        run(pools[2], pools[3])


def adam_of_sources(table, near, far):
    part, cc = near[1].shape[1:]
    specs = [
        [
            pl.BlockSpec((1, 3, part, cc), lambda m, t, r=r: (t[r, m], 0, 0, 0)),
            pl.BlockSpec((1, part, cc), lambda m, t, r=r: (t[r, m], 0, 0)),
        ]
        for r in (1, 2)
    ]
    return pl.pallas_call(
        adam_kernel,
        grid_spec=pltpu.PrefetchScalarGridSpec(
            num_scalar_prefetch=1,
            grid=(8,),
            in_specs=specs[0] + specs[1],
            out_specs=pl.BlockSpec((1, 3, part, cc), lambda m, t: (m, 0, 0, 0)),
        ),
        out_shape=jax.ShapeDtypeStruct((8, 3, part, cc), BF16),
        compiler_params=PARAMS,
        cost_estimate=SMALL,
        name="adam_of_sources",
    )(table, *near, *far)


def crossing(source):
    eight = jnp.arange(8, dtype=jnp.int32)
    src = source.reshape(4, 2, 2).transpose(1, 0, 2).reshape(2, 8)
    cross = (src // 2) % 2 != jnp.arange(2, dtype=jnp.int32)[:, None]
    same = src[:, :, None] == src[:, None, :]
    first_same = jnp.min(jnp.where(same, eight[None, None, :], 8), axis=2)
    is_first = cross & (first_same == eight[None, :])
    before = (eight[None, :] < eight[:, None]).astype(jnp.int32)
    rank = jnp.sum(is_first[:, None, :].astype(jnp.int32) * before[None], axis=2)
    slot = jnp.sum(jnp.where(first_same[:, :, None] == eight, rank[:, None, :], 0), axis=2)
    count = jnp.max(jnp.sum(is_first.astype(jnp.int32), axis=1))
    holds = is_first[:, :, None] & (rank[:, :, None] == eight)
    slot_src = jnp.sum(jnp.where(holds, src[:, :, None], 0), axis=1)
    return src, cross.astype(jnp.int32), slot, slot_src, count


def store_kernel(*refs):
    back_ref, outs = refs[0], refs[-3:]
    cc = back_ref.shape[3]
    for g in range(2):
        for k in range(3):
            outs[k][:, g * cc : (g + 1) * cc] = back_ref[g, k]


def store(outs, back, chunk):
    part, cc = back.shape[2:]
    out_spec = pl.BlockSpec((part, 2 * cc), lambda q: (q, chunk))
    return pl.pallas_call(
        store_kernel,
        grid=(4,),
        in_specs=[pl.BlockSpec((2, 3, part, cc), lambda q: (q, 0, 0, 0))] + [ANYWHERE] * len(outs),
        out_specs=[out_spec] * 3,
        out_shape=[jax.ShapeDtypeStruct((4 * part, 2 * cc * CHUNKS), BF16)] * 3,
        input_output_aliases={1 + k: k for k in range(len(outs))},
        compiler_params=STORE_PARAMS,
        cost_estimate=SMALL,
        name="store",
    )(back, *outs)


def gather_rows(w_ref, own_ref, other_ref):
    rows = own_ref.shape[0]

    @pl.when(pl.program_id(0) == 0)
    def _():
        w_ref[:rows] = own_ref[...]
        w_ref[rows:] = other_ref[...]


def input_grad_kernel(y_ref, *refs):
    *ins, w_ref = refs
    cots, (own_ref, other_ref, x_ref), outs, gain_ref = ins[:-8], ins[-8:-5], ins[-5:-1], ins[-1]
    gather_rows(w_ref, own_ref, other_ref)
    turn = pl.program_id(0)
    total = None
    cut = cots[0].shape[1]
    for i, cot in enumerate(cots):
        term = lax.dot_general(
            cot[...],
            w_ref[:, i * cut : (i + 1) * cut],
            (((1,), (1,)), ((), ())),
            preferred_element_type=F32,
        )
        total = term if total is None else total + term

    for d in range(4):

        @pl.when(turn == d)
        def _():
            outs[d][...] = total.astype(BF16)

    @pl.when(turn == 0)
    def _():
        gain_ref[...] = jnp.zeros_like(gain_ref)

    gain_ref[...] += jnp.sum(total * x_ref[...].astype(F32), axis=0, keepdims=True)


def input_grads(cots, w, x, y):
    count, depth = x.shape
    step = count // 4
    row = lambda i, y_ref: ((y_ref[0] + i) % 4, 0)
    whole = lambda i, y_ref: (0, 0)
    *grads, gain = pl.pallas_call(
        input_grad_kernel,
        grid_spec=pltpu.PrefetchScalarGridSpec(
            num_scalar_prefetch=1,
            grid=(4,),
            in_specs=[pl.BlockSpec((step, c.shape[1]), row) for c in cots]
            + [pl.BlockSpec(half.shape, whole) for half in w]
            + [pl.BlockSpec((step, depth), row)],
            out_specs=[pl.BlockSpec((step, depth), whole)] * 4 + [pl.BlockSpec((1, depth), whole)],
            scratch_shapes=[pltpu.VMEM((depth, w[0].shape[1]), BF16)],
        ),
        out_shape=[jax.ShapeDtypeStruct((step, depth), BF16)] * 4
        + [jax.ShapeDtypeStruct((1, depth), F32)],
        compiler_params=PARAMS,
        cost_estimate=SMALL,
        name="input_grads",
    )(y[None], *cots, *w, x)
    return grads, gain


def value_kernel(y_ref, x_ref, w_own_ref, w_other_ref, *refs):
    *outs, w_ref = refs
    gather_rows(w_ref, w_own_ref, w_other_ref)
    turn = pl.program_id(0)
    part = jnp.dot(x_ref[...], w_ref[...], preferred_element_type=F32).astype(BF16)
    half = part.shape[1] // 2
    for d, out in ((0, outs[0]), (1, outs[1]), (3, outs[4])):

        @pl.when(turn == d)
        def _():
            out[...] = part

    @pl.when(turn == 2)
    def _():
        outs[2][...] = part[:, :half]
        outs[3][...] = part[:, half:]


def value_parts(x, w, y):
    count, depth = x.shape
    width = w[0].shape[1]
    step = count // 4
    whole = lambda i, y_ref: (0, 0)
    widths = [width, width, width // 2, width // 2, width]
    return pl.pallas_call(
        value_kernel,
        grid_spec=pltpu.PrefetchScalarGridSpec(
            num_scalar_prefetch=1,
            grid=(4,),
            in_specs=[pl.BlockSpec((step, depth), lambda i, y_ref: ((y_ref[0] + i) % 4, 0))]
            + [pl.BlockSpec(half.shape, whole) for half in w],
            out_specs=[pl.BlockSpec((step, n), whole) for n in widths],
            scratch_shapes=[pltpu.VMEM((depth, width), BF16)],
        ),
        out_shape=[jax.ShapeDtypeStruct((step, n), BF16) for n in widths],
        compiler_params=PARAMS,
        cost_estimate=SMALL,
        name="value_parts",
    )(y[None], x, *w)


def shards(
    hidden,
    value_grad,
    weight,
    moment_one,
    moment_two,
    norm_gain,
    gain_first,
    gain_second,
    donors,
    recipient,
):
    member = lax.axis_index("member")
    fsdp = lax.axis_index("fsdp")
    z, xl, core = member // 4, (member // 2) % 2, member % 2
    xh, y = fsdp // 4, fsdp % 4
    y_at = [(y + d) % 4 for d in range(4)]
    y_from = [(y - d) % 4 for d in range(4)]

    tokens, features = hidden.shape[1:]
    width = value_grad.shape[2]
    rows = features // 8
    cut = width // CHUNKS

    source = jnp.where(recipient == 1, donors, jnp.arange(16, dtype=jnp.int32))
    src, cross, slot, slot_src, count = crossing(source)
    place = lambda s: s // 4 * 2 + s % 2
    my_src, my_cross, my_slot = pick(src, xl), pick(cross, xl), pick(slot, xl)
    leaving = place(pick(slot_src, 1 - xl))
    table = jnp.stack([my_cross, place(my_src), my_slot])
    table_few = jnp.stack([my_cross, place(my_src), jnp.minimum(my_slot, SLOTS - 1)])

    blocks = split_inputs(hidden[0], norm_gain, xh)
    pieces = [pick(blocks, y_at[d]) for d in (1, 2, 3)]
    arrived = [to_fsdp(piece, dy=d) for d, piece in zip((1, 2, 3), pieces)]
    w_quarter = [weight[0], to_fsdp(weight[0], dx=1)]

    cots = [
        lax.all_gather(
            value_grad[0, :, i * cut : (i + 1) * cut], "fsdp", axis_index_groups=Y_GROUPS, tiled=True
        )
        for i in range(CHUNKS)
    ]

    spread = spread_states([tie(weight[0], pieces), moment_one[0], moment_two[0]])
    held0 = swap_members(spread[0])
    sent = take_pieces(held0, leaving[:SLOTS])
    far_held0 = to_member(sent, dx=1)
    held1 = swap_members(tie(spread[1], sent))
    arrived, inputs, _ = lax.optimization_barrier((arrived, blocks, sent))
    for d in (1, 2, 3):
        inputs = put(inputs, arrived[d - 1], y_from[d])
    inputs = inputs.reshape(4 * tokens, 2 * rows)

    partial0 = matmul(inputs, cots[0], (0, 0)).astype(BF16)

    value_part = value_parts(tie(inputs, partial0), w_quarter, y)

    came0 = tie(to_fsdp(partial0[rows:], dx=1), held1, far_held0, value_part[0])
    sum0 = add_halves(partial0, came0)
    grad0 = swap_members(sum0)
    cots[1] = tie(cots[1], sum0)
    partial1 = matmul(inputs, cots[1], (0, 0)).astype(BF16)

    def many(near, far):
        rest = leaving[SLOTS:]
        more = [to_member(take_pieces(pool, rest), dx=1) for pool in near]
        far = [jnp.concatenate(pair) for pair in zip(far, more)]
        return adam_of_sources(table, near, far)

    def new_states(near, far):
        return lax.cond(
            count > SLOTS, many, lambda near, far: adam_of_sources(table_few, near, far), near, far
        )

    grad0 = tie(grad0, partial1)
    sent = take_pieces(grad0, leaving[:SLOTS])
    far_grad0 = to_member(sent, dx=1)

    input_grad, gain_part = input_grads(cots, w_quarter, tie(inputs, partial1), y)
    value_got = {1: to_fsdp(value_part[1], dy=1), 3: to_fsdp(value_part[4], dy=3)}
    value_got[2] = [to_fsdp(half, dy=2) for half in value_part[2:4]]

    came1 = to_fsdp(partial1[rows:], dx=1)
    came1 = tie(came1, input_grad[0], sent, value_got[1], value_got[3])
    sum1 = add_halves(partial1, came1)
    new0 = new_states([held0, grad0], [far_held0, tie(far_grad0, sum1)])
    grad1 = tie(swap_members(sum1), new0)
    far_held1 = to_member(take_pieces(tie(held1, new0), leaving[:SLOTS]), dx=1)
    back0 = swap_members(tie(new0, grad1, value_got[2][0]))
    sent = take_pieces(grad1, leaving[:SLOTS])
    far_grad1 = tie(to_member(sent, dx=1), value_got[2][1])
    new1 = new_states([held1, grad1], [far_held1, far_grad1])
    back1 = swap_members(new1)

    gain_part = tie(gain_part, sent).reshape(2, rows)
    gain_parts = jnp.zeros((4, 2, rows), F32)
    for d in range(4):
        got = to_fsdp(gain_part, dy=d) if d else gain_part
        gain_parts = put(gain_parts, got, y_from[d])
    grads_got = [to_fsdp(input_grad[d], dy=d) for d in (1, 2, 3)]
    gain_sum = gain_parts + to_fsdp(gain_parts, dx=1)[:, ::-1]
    gain_sum = jnp.where(xh == 0, gain_sum, gain_sum[:, ::-1]).transpose(1, 0, 2)
    gain_grad = gain_sum.reshape(1, features) / (1.0 + norm_gain)
    gain_new = jnp.concatenate(
        adam_update(norm_gain, gain_grad, gain_first, gain_second, 0.0)
    )
    gain_every = lax.all_gather(jnp.pad(gain_new, ((0, 2), (0, 0))), "member")
    gain_all = pick(gain_every, pick(source, member))[:3, None]

    outs = store(store([], back0, 0), back1, 1)

    parts = [input_grad[0]] + grads_got
    value_parts_got = [value_part[0], value_got[1], value_got[3], *value_got[2]]
    hidden_grad, values = join_parts(
        hidden[0], tie(norm_gain, new1), parts, value_parts_got, xh, y
    )
    return (
        values[None],
        hidden_grad[None],
        *(out[None] for out in outs),
        gain_all[0],
        gain_all[1],
        gain_all[2],
    )


def solution(mesh):
    tok = P("member", "fsdp", None)
    mem = P("member", None)
    return jax.shard_map(
        shards,
        mesh=mesh,
        in_specs=(tok,) * 5 + (mem,) * 3 + (P(), P()),
        out_specs=(tok,) * 5 + (mem,) * 3,
        check_vma=False,
    )
```

```python
import functools

import jax
import jax.numpy as jnp
from jax import lax
from jax.experimental import pallas as pl
from jax.experimental.pallas import tpu as pltpu
from jax.sharding import PartitionSpec as P

STEP = 100
beta_one = 0.9
beta_two = 0.999
adam_eps = 1e-08
learn_rate = 0.001
decay_rate = 0.1
norm_eps = 1e-06

BF16 = jnp.bfloat16
F32 = jnp.float32
CHUNKS = 2
SLOTS = 3

Y_GROUPS = [[0, 1, 2, 3], [4, 5, 6, 7]]
X_GROUPS = [[p // 2 * 4 + x * 2 + p % 2 for p in range(8)] for x in range(2)]
PARAMS = pltpu.CompilerParams(vmem_limit_bytes=56 * 1024 * 1024)
STORE_PARAMS = pltpu.CompilerParams(vmem_limit_bytes=16 * 1024 * 1024)


def adam_update(param, grad, first, second, decay):
    first_new = beta_one * first + (1.0 - beta_one) * grad
    second_new = beta_two * second + (1.0 - beta_two) * grad * grad
    corr_one = 1.0 - beta_one**STEP
    corr_two = 1.0 - beta_two**STEP
    step_dir = first_new / corr_one / (jnp.sqrt(second_new / corr_two) + adam_eps) + decay * param
    return (param - learn_rate * step_dir, first_new, second_new)


def to_fsdp(x, dx=0, dy=0):
    pairs = [(f, ((f // 4) ^ dx) * 4 + (f % 4 + dy) % 4) for f in range(8)]
    return lax.ppermute(x, "fsdp", pairs)


def to_member(x, dz=0, dx=0, dc=0):
    pairs = [
        (m, ((m // 4 + dz) % 4) * 4 + ((m // 2 % 2) ^ dx) * 2 + ((m % 2) ^ dc)) for m in range(16)
    ]
    return lax.ppermute(x, "member", pairs)


def swap_members(x):
    return lax.all_to_all(x, "member", 0, 0, axis_index_groups=X_GROUPS)


def pick(x, index, axis=0):
    return lax.dynamic_index_in_dim(x, index, axis, keepdims=False)


def tie(x, *others):
    return lax.optimization_barrier((x, others))[0]


def put(x, part, index, axis=0):
    return lax.dynamic_update_index_in_dim(x, part, index, axis)


def matmul(a, b, contract):
    return lax.dot_general(a, b, ((contract[:1], contract[1:]), ((), ())), preferred_element_type=F32)


SMALL = pl.CostEstimate(flops=0, bytes_accessed=65536, transcendentals=0)
LARGE = pl.CostEstimate(flops=20_000_000_000, bytes_accessed=10_000_000, transcendentals=0)
ANYWHERE = pl.BlockSpec(memory_space=pl.ANY)


def split_kernel(xh_ref, hidden_ref, gain_ref, out_ref):
    wide = hidden_ref[...].astype(F32)
    scale = lax.rsqrt(jnp.mean(wide * wide, axis=-1, keepdims=True) + norm_eps)
    full = wide * scale * (1.0 + gain_ref[...])
    half = full.shape[1] // 2
    rows = half // 4
    low, high = full[:, :half], full[:, half:]
    swap = xh_ref[0] == 1
    first, second = jnp.where(swap, high, low), jnp.where(swap, low, high)
    for q in range(4):
        part = slice(q * rows, (q + 1) * rows)
        out_ref[q] = jnp.concatenate([first[:, part], second[:, part]], axis=1).astype(BF16)


def split_inputs(hidden, gain, xh):
    tokens, features = hidden.shape
    step = 96
    return pl.pallas_call(
        split_kernel,
        grid_spec=pltpu.PrefetchScalarGridSpec(
            num_scalar_prefetch=1,
            grid=(tokens // step,),
            in_specs=[
                pl.BlockSpec((step, features), lambda i, s: (i, 0)),
                pl.BlockSpec((1, features), lambda i, s: (0, 0)),
            ],
            out_specs=pl.BlockSpec((4, step, features // 4), lambda i, s: (0, i, 0)),
        ),
        out_shape=jax.ShapeDtypeStruct((4, tokens, features // 4), BF16),
        compiler_params=PARAMS,
        cost_estimate=SMALL,
        name="split_inputs",
    )(xh[None], hidden, gain)


def join_kernel(place_ref, hidden_ref, gain_ref, *refs):
    ins, value_refs, (out_ref, values_ref) = refs[:4], refs[4:9], refs[9:]
    xh, y = place_ref[0], place_ref[1]
    total = value_refs[0][...].astype(F32)
    for ref in value_refs[1:3]:
        total = total + ref[...].astype(F32)
    half = total.shape[1] // 2
    for k, ref in enumerate(value_refs[3:]):
        at = slice(k * half, (k + 1) * half)
        values_ref[:, at] = (total[:, at] + ref[...].astype(F32)).astype(BF16)
    wide = hidden_ref[...].astype(F32)
    scale = lax.rsqrt(jnp.mean(wide * wide, axis=-1, keepdims=True) + norm_eps)
    normed = wide * scale
    rows = ins[0].shape[1] // 2
    came = [ref[...].astype(F32) for ref in ins]
    parts = []
    for q in range(4):
        d = lax.rem(y + (4 - q), 4)
        part = came[0]
        for k in (1, 2, 3):
            part = jnp.where(d == k, came[k], part)
        parts.append(part)
    first = jnp.concatenate([p[:, :rows] for p in parts], axis=1)
    second = jnp.concatenate([p[:, rows:] for p in parts], axis=1)
    swap = xh == 1
    grad = jnp.concatenate([jnp.where(swap, second, first), jnp.where(swap, first, second)], axis=1)
    scaled = grad * (1.0 + gain_ref[...])
    mean = jnp.mean(scaled * normed, axis=-1, keepdims=True)
    out_ref[...] = (scale * (scaled - normed * mean)).astype(BF16)


def join_parts(hidden, gain, parts, values, xh, y):
    tokens, features = hidden.shape
    step = 96
    row = lambda i, s: (i, 0)
    return pl.pallas_call(
        join_kernel,
        grid_spec=pltpu.PrefetchScalarGridSpec(
            num_scalar_prefetch=1,
            grid=(tokens // step,),
            in_specs=[
                pl.BlockSpec((step, features), row),
                pl.BlockSpec((1, features), lambda i, s: (0, 0)),
            ]
            + [pl.BlockSpec((step, features // 4), row)] * 4
            + [pl.BlockSpec((step, value.shape[1]), row) for value in values],
            out_specs=[
                pl.BlockSpec((step, features), row),
                pl.BlockSpec((step, values[0].shape[1]), row),
            ],
        ),
        out_shape=[
            jax.ShapeDtypeStruct((tokens, features), BF16),
            jax.ShapeDtypeStruct(values[0].shape, BF16),
        ],
        compiler_params=PARAMS,
        cost_estimate=LARGE,
        name="join_parts",
    )(jnp.stack([xh, y]), hidden, gain, *parts, *values)


def spread_kernel(*refs):
    ins, outs = refs[:3], refs[3:]
    cc = outs[0].shape[3]
    for i, out_ref in enumerate(outs):
        for g in range(2):
            at = (2 * i + g) * cc
            for k in range(3):
                out_ref[g, k] = ins[k][:, at : at + cc]


def spread_states(arrays):
    rows, width = arrays[0].shape
    part, cc = rows // 4, width // CHUNKS // 2
    return pl.pallas_call(
        spread_kernel,
        grid=(4,),
        in_specs=[pl.BlockSpec((part, width), lambda q: (q, 0))] * 3,
        out_specs=[pl.BlockSpec((2, 3, part, cc), lambda q: (q, 0, 0, 0))] * CHUNKS,
        out_shape=[jax.ShapeDtypeStruct((8, 3, part, cc), BF16)] * CHUNKS,
        compiler_params=PARAMS,
        cost_estimate=SMALL,
        name="spread_states",
    )(*arrays)


def add_kernel(here_ref, came_ref, out_ref):
    cc = out_ref.shape[2]
    for g in range(2):
        at = slice(g * cc, (g + 1) * cc)
        out_ref[g] = (here_ref[:, at].astype(F32) + came_ref[:, at].astype(F32)).astype(BF16)


def add_halves(here, came):
    rows, cut = came.shape
    part = rows // 4
    return pl.pallas_call(
        add_kernel,
        grid=(4,),
        in_specs=[pl.BlockSpec((part, cut), lambda q: (q, 0))] * 2,
        out_specs=pl.BlockSpec((2, part, cut // 2), lambda q: (q, 0, 0)),
        out_shape=jax.ShapeDtypeStruct((8, part, cut // 2), BF16),
        compiler_params=PARAMS,
        cost_estimate=SMALL,
        name="add_halves",
    )(here, came)


def take_pieces(pool, places):
    number, block = places.shape[0], pool.shape[1:]

    def kernel(places_ref, pool_ref, out_ref, buffers, sems):
        loads = [
            pltpu.make_async_copy(pool_ref.at[places_ref[j]], buffers.at[j], sems.at[0, j])
            for j in range(number)
        ]
        stores = [
            pltpu.make_async_copy(buffers.at[j], out_ref.at[j], sems.at[1, j]) for j in range(number)
        ]
        for load in loads:
            load.start()
        for load, back in zip(loads, stores):
            load.wait()
            back.start()
        for back in stores:
            back.wait()

    return pl.pallas_call(
        kernel,
        in_specs=[pl.BlockSpec(memory_space=pltpu.SMEM), ANYWHERE],
        out_specs=ANYWHERE,
        out_shape=jax.ShapeDtypeStruct((number,) + block, BF16),
        scratch_shapes=[pltpu.VMEM((number,) + block, BF16), pltpu.SemaphoreType.DMA((2, number))],
        compiler_params=PARAMS,
        cost_estimate=SMALL,
        name="take_pieces",
    )(places, pool)


def put_blocks(blocks, parts, places):
    number, block = len(parts), parts[0].shape

    def kernel(places_ref, *refs):
        out_ref, buffers, sems = refs[number + 1 :]
        loads = [
            pltpu.make_async_copy(refs[k], buffers.at[k], sems.at[0, k]) for k in range(number)
        ]
        stores = [
            pltpu.make_async_copy(buffers.at[k], out_ref.at[places_ref[k]], sems.at[1, k])
            for k in range(number)
        ]
        for load in loads:
            load.start()
        for load, back in zip(loads, stores):
            load.wait()
            back.start()
        for back in stores:
            back.wait()

    return pl.pallas_call(
        kernel,
        in_specs=[pl.BlockSpec(memory_space=pltpu.SMEM)] + [ANYWHERE] * (number + 1),
        out_specs=ANYWHERE,
        out_shape=jax.ShapeDtypeStruct(blocks.shape, BF16),
        input_output_aliases={number + 1: 0},
        scratch_shapes=[pltpu.VMEM((number,) + block, BF16), pltpu.SemaphoreType.DMA((2, number))],
        compiler_params=PARAMS,
        cost_estimate=SMALL,
        name="put_blocks",
    )(places, *parts, blocks)


def adam_kernel(table_ref, *refs):
    pools, out_ref = refs[:4], refs[4]
    step = 16

    def run(held_ref, grad_ref):
        for i in range(grad_ref.shape[1] // step):
            at = slice(i * step, (i + 1) * step)
            state = [held_ref[0, k, at, :].astype(F32) for k in range(3)]
            grad = grad_ref[0, at, :].astype(F32)
            new = adam_update(state[0], grad, state[1], state[2], decay_rate)
            for k in range(3):
                out_ref[0, k, at, :] = new[k].astype(BF16)

    far = table_ref[0, pl.program_id(0)]

    @pl.when(far == 0)
    def _():
        run(pools[0], pools[1])

    @pl.when(far == 1)
    def _():
        run(pools[2], pools[3])


def adam_of_sources(table, near, far):
    part, cc = near[1].shape[1:]
    specs = [
        [
            pl.BlockSpec((1, 3, part, cc), lambda m, t, r=r: (t[r, m], 0, 0, 0)),
            pl.BlockSpec((1, part, cc), lambda m, t, r=r: (t[r, m], 0, 0)),
        ]
        for r in (1, 2)
    ]
    return pl.pallas_call(
        adam_kernel,
        grid_spec=pltpu.PrefetchScalarGridSpec(
            num_scalar_prefetch=1,
            grid=(8,),
            in_specs=specs[0] + specs[1],
            out_specs=pl.BlockSpec((1, 3, part, cc), lambda m, t: (m, 0, 0, 0)),
        ),
        out_shape=jax.ShapeDtypeStruct((8, 3, part, cc), BF16),
        compiler_params=PARAMS,
        cost_estimate=SMALL,
        name="adam_of_sources",
    )(table, *near, *far)


def crossing(source):
    eight = jnp.arange(8, dtype=jnp.int32)
    src = source.reshape(4, 2, 2).transpose(1, 0, 2).reshape(2, 8)
    cross = (src // 2) % 2 != jnp.arange(2, dtype=jnp.int32)[:, None]
    same = src[:, :, None] == src[:, None, :]
    first_same = jnp.min(jnp.where(same, eight[None, None, :], 8), axis=2)
    is_first = cross & (first_same == eight[None, :])
    before = (eight[None, :] < eight[:, None]).astype(jnp.int32)
    rank = jnp.sum(is_first[:, None, :].astype(jnp.int32) * before[None], axis=2)
    slot = jnp.sum(jnp.where(first_same[:, :, None] == eight, rank[:, None, :], 0), axis=2)
    count = jnp.max(jnp.sum(is_first.astype(jnp.int32), axis=1))
    holds = is_first[:, :, None] & (rank[:, :, None] == eight)
    slot_src = jnp.sum(jnp.where(holds, src[:, :, None], 0), axis=1)
    return src, cross.astype(jnp.int32), slot, slot_src, count


def store_kernel(*refs):
    back_ref, outs = refs[0], refs[-3:]
    cc = back_ref.shape[3]
    for g in range(2):
        for k in range(3):
            outs[k][:, g * cc : (g + 1) * cc] = back_ref[g, k]


def store(outs, back, chunk):
    part, cc = back.shape[2:]
    out_spec = pl.BlockSpec((part, 2 * cc), lambda q: (q, chunk))
    return pl.pallas_call(
        store_kernel,
        grid=(4,),
        in_specs=[pl.BlockSpec((2, 3, part, cc), lambda q: (q, 0, 0, 0))] + [ANYWHERE] * len(outs),
        out_specs=[out_spec] * 3,
        out_shape=[jax.ShapeDtypeStruct((4 * part, 2 * cc * CHUNKS), BF16)] * 3,
        input_output_aliases={1 + k: k for k in range(len(outs))},
        compiler_params=STORE_PARAMS,
        cost_estimate=SMALL,
        name="store",
    )(back, *outs)


def gather_rows(w_ref, own_ref, other_ref):
    rows = own_ref.shape[0]

    @pl.when(pl.program_id(0) == 0)
    def _():
        w_ref[:rows] = own_ref[...]
        w_ref[rows:] = other_ref[...]


def input_grad_kernel(y_ref, *refs):
    *ins, w_ref = refs
    cots, (own_ref, other_ref, x_ref), outs, gain_ref = ins[:-8], ins[-8:-5], ins[-5:-1], ins[-1]
    gather_rows(w_ref, own_ref, other_ref)
    turn = pl.program_id(0)
    total = None
    cut = cots[0].shape[1]
    for i, cot in enumerate(cots):
        term = lax.dot_general(
            cot[...],
            w_ref[:, i * cut : (i + 1) * cut],
            (((1,), (1,)), ((), ())),
            preferred_element_type=F32,
        )
        total = term if total is None else total + term

    for d in range(4):

        @pl.when(turn == d)
        def _():
            outs[d][...] = total.astype(BF16)

    @pl.when(turn == 0)
    def _():
        gain_ref[...] = jnp.zeros_like(gain_ref)

    gain_ref[...] += jnp.sum(total * x_ref[...].astype(F32), axis=0, keepdims=True)


def input_grads(cots, w, x, y):
    count, depth = x.shape
    step = count // 4
    row = lambda i, y_ref: ((y_ref[0] + i) % 4, 0)
    whole = lambda i, y_ref: (0, 0)
    *grads, gain = pl.pallas_call(
        input_grad_kernel,
        grid_spec=pltpu.PrefetchScalarGridSpec(
            num_scalar_prefetch=1,
            grid=(4,),
            in_specs=[pl.BlockSpec((step, c.shape[1]), row) for c in cots]
            + [pl.BlockSpec(half.shape, whole) for half in w]
            + [pl.BlockSpec((step, depth), row)],
            out_specs=[pl.BlockSpec((step, depth), whole)] * 4 + [pl.BlockSpec((1, depth), whole)],
            scratch_shapes=[pltpu.VMEM((depth, w[0].shape[1]), BF16)],
        ),
        out_shape=[jax.ShapeDtypeStruct((step, depth), BF16)] * 4
        + [jax.ShapeDtypeStruct((1, depth), F32)],
        compiler_params=PARAMS,
        cost_estimate=SMALL,
        name="input_grads",
    )(y[None], *cots, *w, x)
    return grads, gain


def value_kernel(y_ref, x_ref, w_own_ref, w_other_ref, *refs):
    *outs, w_ref = refs
    gather_rows(w_ref, w_own_ref, w_other_ref)
    turn = pl.program_id(0)
    part = jnp.dot(x_ref[...], w_ref[...], preferred_element_type=F32).astype(BF16)
    half = part.shape[1] // 2
    for d, out in ((0, outs[0]), (1, outs[1]), (3, outs[4])):

        @pl.when(turn == d)
        def _():
            out[...] = part

    @pl.when(turn == 2)
    def _():
        outs[2][...] = part[:, :half]
        outs[3][...] = part[:, half:]


def value_parts(x, w, y):
    count, depth = x.shape
    width = w[0].shape[1]
    step = count // 4
    whole = lambda i, y_ref: (0, 0)
    widths = [width, width, width // 2, width // 2, width]
    return pl.pallas_call(
        value_kernel,
        grid_spec=pltpu.PrefetchScalarGridSpec(
            num_scalar_prefetch=1,
            grid=(4,),
            in_specs=[pl.BlockSpec((step, depth), lambda i, y_ref: ((y_ref[0] + i) % 4, 0))]
            + [pl.BlockSpec(half.shape, whole) for half in w],
            out_specs=[pl.BlockSpec((step, n), whole) for n in widths],
            scratch_shapes=[pltpu.VMEM((depth, width), BF16)],
        ),
        out_shape=[jax.ShapeDtypeStruct((step, n), BF16) for n in widths],
        compiler_params=PARAMS,
        cost_estimate=SMALL,
        name="value_parts",
    )(y[None], x, *w)


def shards(
    hidden,
    value_grad,
    weight,
    moment_one,
    moment_two,
    norm_gain,
    gain_first,
    gain_second,
    donors,
    recipient,
):
    member = lax.axis_index("member")
    fsdp = lax.axis_index("fsdp")
    z, xl, core = member // 4, (member // 2) % 2, member % 2
    xh, y = fsdp // 4, fsdp % 4
    y_at = [(y + d) % 4 for d in range(4)]
    y_from = [(y - d) % 4 for d in range(4)]

    tokens, features = hidden.shape[1:]
    width = value_grad.shape[2]
    rows = features // 8
    cut = width // CHUNKS

    source = jnp.where(recipient == 1, donors, jnp.arange(16, dtype=jnp.int32))
    src, cross, slot, slot_src, count = crossing(source)
    place = lambda s: s // 4 * 2 + s % 2
    my_src, my_cross, my_slot = pick(src, xl), pick(cross, xl), pick(slot, xl)
    leaving = place(pick(slot_src, 1 - xl))
    table = jnp.stack([my_cross, place(my_src), my_slot])
    table_few = jnp.stack([my_cross, place(my_src), jnp.minimum(my_slot, SLOTS - 1)])

    blocks = split_inputs(hidden[0], norm_gain, xh)
    pieces = [pick(blocks, y_at[d]) for d in (1, 2, 3)]
    arrived = [to_fsdp(piece, dy=d) for d, piece in zip((1, 2, 3), pieces)]
    w_quarter = [weight[0], to_fsdp(weight[0], dx=1)]

    cots = [
        lax.all_gather(
            value_grad[0, :, i * cut : (i + 1) * cut], "fsdp", axis_index_groups=Y_GROUPS, tiled=True
        )
        for i in range(CHUNKS)
    ]

    spread = spread_states([tie(weight[0], pieces), moment_one[0], moment_two[0]])
    held0 = swap_members(spread[0])
    sent = take_pieces(held0, leaving[:SLOTS])
    far_held0 = to_member(sent, dx=1)
    arrived, blocks, w_quarter, _ = lax.optimization_barrier((arrived, blocks, w_quarter, sent))
    inputs = put_blocks(blocks, arrived, jnp.stack(y_from[1:])).reshape(4 * tokens, 2 * rows)

    partial0 = matmul(inputs, cots[0], (0, 0)).astype(BF16)
    held1 = swap_members(tie(spread[1], partial0, far_held0))

    value_part = value_parts(tie(inputs, partial0), w_quarter, y)

    came0 = tie(to_fsdp(partial0[rows:], dx=1), far_held0, value_part[0])
    sum0 = add_halves(partial0, came0)
    cots[1] = tie(cots[1], sum0)
    partial1 = matmul(inputs, cots[1], (0, 0)).astype(BF16)

    def many(near, far):
        rest = leaving[SLOTS:]
        more = [to_member(take_pieces(pool, rest), dx=1) for pool in near]
        far = [jnp.concatenate(pair) for pair in zip(far, more)]
        return adam_of_sources(table, near, far)

    def new_states(near, far):
        return lax.cond(
            count > SLOTS, many, lambda near, far: adam_of_sources(table_few, near, far), near, far
        )

    grad0 = swap_members(tie(sum0, held1, partial1))
    sent = take_pieces(grad0, leaving[:SLOTS])
    far_grad0 = to_member(sent, dx=1)

    input_grad, gain_part = input_grads(cots, w_quarter, tie(inputs, partial1), y)
    value_got = {1: to_fsdp(value_part[1], dy=1), 3: to_fsdp(value_part[4], dy=3)}
    value_got[2] = [to_fsdp(half, dy=2) for half in value_part[2:4]]

    came1 = to_fsdp(partial1[rows:], dx=1)
    came1 = tie(came1, input_grad[0], sent, value_got[1], value_got[3])
    sum1 = add_halves(partial1, came1)
    new0 = new_states([held0, grad0], [far_held0, tie(far_grad0, sum1)])
    grad1 = tie(swap_members(sum1), new0)
    far_held1 = to_member(take_pieces(tie(held1, new0), leaving[:SLOTS]), dx=1)
    back0 = swap_members(tie(new0, grad1, value_got[2][0]))
    sent = take_pieces(grad1, leaving[:SLOTS])
    far_grad1 = to_member(tie(sent, far_held1), dx=1)
    new1 = new_states([held1, grad1], [far_held1, tie(far_grad1, value_got[2][1])])
    back1 = swap_members(new1)

    gain_part = tie(gain_part, sent).reshape(2, rows)
    gain_parts = jnp.zeros((4, 2, rows), F32)
    for d in range(4):
        got = to_fsdp(gain_part, dy=d) if d else gain_part
        gain_parts = put(gain_parts, got, y_from[d])
    grads_got = [to_fsdp(tie(input_grad[d], far_grad1), dy=d) for d in (1, 2, 3)]
    gain_sum = gain_parts + to_fsdp(gain_parts, dx=1)[:, ::-1]
    gain_sum = jnp.where(xh == 0, gain_sum, gain_sum[:, ::-1]).transpose(1, 0, 2)
    gain_grad = gain_sum.reshape(1, features) / (1.0 + norm_gain)
    gain_new = jnp.concatenate(
        adam_update(norm_gain, gain_grad, gain_first, gain_second, 0.0)
    )
    gain_every = lax.all_gather(jnp.pad(gain_new, ((0, 2), (0, 0))), "member")
    gain_all = pick(gain_every, pick(source, member))[:3, None]

    outs = store(store([], back0, 0), back1, 1)

    parts = [input_grad[0]] + grads_got
    value_parts_got = [value_part[0], value_got[1], value_got[3], *value_got[2]]
    hidden_grad, values = join_parts(
        hidden[0], tie(norm_gain, new1), parts, value_parts_got, xh, y
    )
    return (
        values[None],
        hidden_grad[None],
        *(out[None] for out in outs),
        gain_all[0],
        gain_all[1],
        gain_all[2],
    )


def solution(mesh):
    tok = P("member", "fsdp", None)
    mem = P("member", None)
    return jax.shard_map(
        shards,
        mesh=mesh,
        in_specs=(tok,) * 5 + (mem,) * 3 + (P(), P()),
        out_specs=(tok,) * 5 + (mem,) * 3,
        check_vma=False,
    )
```

```python
import functools

import jax
import jax.numpy as jnp
from jax import lax
from jax.experimental import pallas as pl
from jax.experimental.pallas import tpu as pltpu
from jax.sharding import PartitionSpec as P

STEP = 100
beta_one = 0.9
beta_two = 0.999
adam_eps = 1e-08
learn_rate = 0.001
decay_rate = 0.1
norm_eps = 1e-06

BF16 = jnp.bfloat16
F32 = jnp.float32
CHUNKS = 2
SLOTS = 3

Y_GROUPS = [[0, 1, 2, 3], [4, 5, 6, 7]]
X_GROUPS = [[p // 2 * 4 + x * 2 + p % 2 for p in range(8)] for x in range(2)]
PARAMS = pltpu.CompilerParams(vmem_limit_bytes=56 * 1024 * 1024)
STORE_PARAMS = pltpu.CompilerParams(vmem_limit_bytes=16 * 1024 * 1024)


def adam_update(param, grad, first, second, decay):
    first_new = beta_one * first + (1.0 - beta_one) * grad
    second_new = beta_two * second + (1.0 - beta_two) * grad * grad
    corr_one = 1.0 - beta_one**STEP
    corr_two = 1.0 - beta_two**STEP
    scaled = jnp.sqrt(second_new * (1.0 / corr_two)) + adam_eps
    step_dir = first_new * (1.0 / corr_one) / scaled + decay * param
    return (param - learn_rate * step_dir, first_new, second_new)


def to_fsdp(x, dx=0, dy=0):
    pairs = [(f, ((f // 4) ^ dx) * 4 + (f % 4 + dy) % 4) for f in range(8)]
    return lax.ppermute(x, "fsdp", pairs)


def to_member(x, dz=0, dx=0, dc=0):
    pairs = [
        (m, ((m // 4 + dz) % 4) * 4 + ((m // 2 % 2) ^ dx) * 2 + ((m % 2) ^ dc)) for m in range(16)
    ]
    return lax.ppermute(x, "member", pairs)


def swap_members(x):
    return lax.all_to_all(x, "member", 0, 0, axis_index_groups=X_GROUPS)


def pick(x, index, axis=0):
    return lax.dynamic_index_in_dim(x, index, axis, keepdims=False)


def tie(x, *others):
    return lax.optimization_barrier((x, others))[0]


def put(x, part, index, axis=0):
    return lax.dynamic_update_index_in_dim(x, part, index, axis)


def matmul(a, b, contract):
    return lax.dot_general(a, b, ((contract[:1], contract[1:]), ((), ())), preferred_element_type=F32)


SMALL = pl.CostEstimate(flops=0, bytes_accessed=65536, transcendentals=0)
LARGE = pl.CostEstimate(flops=20_000_000_000, bytes_accessed=10_000_000, transcendentals=0)
ANYWHERE = pl.BlockSpec(memory_space=pl.ANY)


def split_kernel(xh_ref, hidden_ref, gain_ref, out_ref):
    wide = hidden_ref[...].astype(F32)
    scale = lax.rsqrt(jnp.mean(wide * wide, axis=-1, keepdims=True) + norm_eps)
    full = wide * scale * (1.0 + gain_ref[...])
    half = full.shape[1] // 2
    rows = half // 4
    low, high = full[:, :half], full[:, half:]
    swap = xh_ref[0] == 1
    first, second = jnp.where(swap, high, low), jnp.where(swap, low, high)
    for q in range(4):
        part = slice(q * rows, (q + 1) * rows)
        out_ref[q] = jnp.concatenate([first[:, part], second[:, part]], axis=1).astype(BF16)


def split_inputs(hidden, gain, xh):
    tokens, features = hidden.shape
    step = 96
    return pl.pallas_call(
        split_kernel,
        grid_spec=pltpu.PrefetchScalarGridSpec(
            num_scalar_prefetch=1,
            grid=(tokens // step,),
            in_specs=[
                pl.BlockSpec((step, features), lambda i, s: (i, 0)),
                pl.BlockSpec((1, features), lambda i, s: (0, 0)),
            ],
            out_specs=pl.BlockSpec((4, step, features // 4), lambda i, s: (0, i, 0)),
        ),
        out_shape=jax.ShapeDtypeStruct((4, tokens, features // 4), BF16),
        compiler_params=PARAMS,
        cost_estimate=SMALL,
        name="split_inputs",
    )(xh[None], hidden, gain)


def join_kernel(place_ref, hidden_ref, gain_ref, *refs):
    ins, value_refs, (out_ref, values_ref) = refs[:4], refs[4:9], refs[9:]
    xh, y = place_ref[0], place_ref[1]
    total = value_refs[0][...].astype(F32)
    for ref in value_refs[1:3]:
        total = total + ref[...].astype(F32)
    half = total.shape[1] // 2
    for k, ref in enumerate(value_refs[3:]):
        at = slice(k * half, (k + 1) * half)
        values_ref[:, at] = (total[:, at] + ref[...].astype(F32)).astype(BF16)
    wide = hidden_ref[...].astype(F32)
    scale = lax.rsqrt(jnp.mean(wide * wide, axis=-1, keepdims=True) + norm_eps)
    normed = wide * scale
    rows = ins[0].shape[1] // 2
    came = [ref[...].astype(F32) for ref in ins]
    parts = []
    for q in range(4):
        d = lax.rem(y + (4 - q), 4)
        part = came[0]
        for k in (1, 2, 3):
            part = jnp.where(d == k, came[k], part)
        parts.append(part)
    first = jnp.concatenate([p[:, :rows] for p in parts], axis=1)
    second = jnp.concatenate([p[:, rows:] for p in parts], axis=1)
    swap = xh == 1
    grad = jnp.concatenate([jnp.where(swap, second, first), jnp.where(swap, first, second)], axis=1)
    scaled = grad * (1.0 + gain_ref[...])
    mean = jnp.mean(scaled * normed, axis=-1, keepdims=True)
    out_ref[...] = (scale * (scaled - normed * mean)).astype(BF16)


def join_parts(hidden, gain, parts, values, xh, y):
    tokens, features = hidden.shape
    step = 96
    row = lambda i, s: (i, 0)
    return pl.pallas_call(
        join_kernel,
        grid_spec=pltpu.PrefetchScalarGridSpec(
            num_scalar_prefetch=1,
            grid=(tokens // step,),
            in_specs=[
                pl.BlockSpec((step, features), row),
                pl.BlockSpec((1, features), lambda i, s: (0, 0)),
            ]
            + [pl.BlockSpec((step, features // 4), row)] * 4
            + [pl.BlockSpec((step, value.shape[1]), row) for value in values],
            out_specs=[
                pl.BlockSpec((step, features), row),
                pl.BlockSpec((step, values[0].shape[1]), row),
            ],
        ),
        out_shape=[
            jax.ShapeDtypeStruct((tokens, features), BF16),
            jax.ShapeDtypeStruct(values[0].shape, BF16),
        ],
        compiler_params=PARAMS,
        cost_estimate=LARGE,
        name="join_parts",
    )(jnp.stack([xh, y]), hidden, gain, *parts, *values)


def spread_kernel(*refs):
    ins, outs = refs[:3], refs[3:]
    cc = outs[0].shape[3]
    for i, out_ref in enumerate(outs):
        for g in range(2):
            at = (2 * i + g) * cc
            for k in range(3):
                out_ref[g, k] = ins[k][:, at : at + cc]


def spread_states(arrays):
    rows, width = arrays[0].shape
    part, cc = rows // 4, width // CHUNKS // 2
    return pl.pallas_call(
        spread_kernel,
        grid=(4,),
        in_specs=[pl.BlockSpec((part, width), lambda q: (q, 0))] * 3,
        out_specs=[pl.BlockSpec((2, 3, part, cc), lambda q: (q, 0, 0, 0))] * CHUNKS,
        out_shape=[jax.ShapeDtypeStruct((8, 3, part, cc), BF16)] * CHUNKS,
        compiler_params=PARAMS,
        cost_estimate=SMALL,
        name="spread_states",
    )(*arrays)


def add_kernel(here_ref, came_ref, out_ref):
    cc = out_ref.shape[2]
    for g in range(2):
        at = slice(g * cc, (g + 1) * cc)
        out_ref[g] = (here_ref[:, at].astype(F32) + came_ref[:, at].astype(F32)).astype(BF16)


def add_halves(here, came):
    rows, cut = came.shape
    part = rows // 4
    return pl.pallas_call(
        add_kernel,
        grid=(4,),
        in_specs=[pl.BlockSpec((part, cut), lambda q: (q, 0))] * 2,
        out_specs=pl.BlockSpec((2, part, cut // 2), lambda q: (q, 0, 0)),
        out_shape=jax.ShapeDtypeStruct((8, part, cut // 2), BF16),
        compiler_params=PARAMS,
        cost_estimate=SMALL,
        name="add_halves",
    )(here, came)


def take_pieces(pool, places):
    number, block = places.shape[0], pool.shape[1:]

    def kernel(places_ref, pool_ref, out_ref, buffers, sems):
        loads = [
            pltpu.make_async_copy(pool_ref.at[places_ref[j]], buffers.at[j], sems.at[0, j])
            for j in range(number)
        ]
        stores = [
            pltpu.make_async_copy(buffers.at[j], out_ref.at[j], sems.at[1, j]) for j in range(number)
        ]
        for load in loads:
            load.start()
        for load, back in zip(loads, stores):
            load.wait()
            back.start()
        for back in stores:
            back.wait()

    return pl.pallas_call(
        kernel,
        in_specs=[pl.BlockSpec(memory_space=pltpu.SMEM), ANYWHERE],
        out_specs=ANYWHERE,
        out_shape=jax.ShapeDtypeStruct((number,) + block, BF16),
        scratch_shapes=[pltpu.VMEM((number,) + block, BF16), pltpu.SemaphoreType.DMA((2, number))],
        compiler_params=PARAMS,
        cost_estimate=SMALL,
        name="take_pieces",
    )(places, pool)


def put_blocks(blocks, parts, places):
    number, block = len(parts), parts[0].shape

    def kernel(places_ref, *refs):
        out_ref, buffers, sems = refs[number + 1 :]
        loads = [
            pltpu.make_async_copy(refs[k], buffers.at[k], sems.at[0, k]) for k in range(number)
        ]
        stores = [
            pltpu.make_async_copy(buffers.at[k], out_ref.at[places_ref[k]], sems.at[1, k])
            for k in range(number)
        ]
        for load in loads:
            load.start()
        for load, back in zip(loads, stores):
            load.wait()
            back.start()
        for back in stores:
            back.wait()

    return pl.pallas_call(
        kernel,
        in_specs=[pl.BlockSpec(memory_space=pltpu.SMEM)] + [ANYWHERE] * (number + 1),
        out_specs=ANYWHERE,
        out_shape=jax.ShapeDtypeStruct(blocks.shape, BF16),
        input_output_aliases={number + 1: 0},
        scratch_shapes=[pltpu.VMEM((number,) + block, BF16), pltpu.SemaphoreType.DMA((2, number))],
        compiler_params=PARAMS,
        cost_estimate=SMALL,
        name="put_blocks",
    )(places, *parts, blocks)


def adam_kernel(table_ref, *refs):
    pools, out_ref = refs[:4], refs[4]
    step = 16

    def run(held_ref, grad_ref):
        for i in range(grad_ref.shape[1] // step):
            at = slice(i * step, (i + 1) * step)
            state = [held_ref[0, k, at, :].astype(F32) for k in range(3)]
            grad = grad_ref[0, at, :].astype(F32)
            new = adam_update(state[0], grad, state[1], state[2], decay_rate)
            for k in range(3):
                out_ref[0, k, at, :] = new[k].astype(BF16)

    far = table_ref[0, pl.program_id(0)]

    @pl.when(far == 0)
    def _():
        run(pools[0], pools[1])

    @pl.when(far == 1)
    def _():
        run(pools[2], pools[3])


def adam_of_sources(table, near, far):
    part, cc = near[1].shape[1:]
    specs = [
        [
            pl.BlockSpec((1, 3, part, cc), lambda m, t, r=r: (t[r, m], 0, 0, 0)),
            pl.BlockSpec((1, part, cc), lambda m, t, r=r: (t[r, m], 0, 0)),
        ]
        for r in (1, 2)
    ]
    return pl.pallas_call(
        adam_kernel,
        grid_spec=pltpu.PrefetchScalarGridSpec(
            num_scalar_prefetch=1,
            grid=(8,),
            in_specs=specs[0] + specs[1],
            out_specs=pl.BlockSpec((1, 3, part, cc), lambda m, t: (m, 0, 0, 0)),
        ),
        out_shape=jax.ShapeDtypeStruct((8, 3, part, cc), BF16),
        compiler_params=PARAMS,
        cost_estimate=SMALL,
        name="adam_of_sources",
    )(table, *near, *far)


def crossing(source):
    eight = jnp.arange(8, dtype=jnp.int32)
    src = source.reshape(4, 2, 2).transpose(1, 0, 2).reshape(2, 8)
    cross = (src // 2) % 2 != jnp.arange(2, dtype=jnp.int32)[:, None]
    same = src[:, :, None] == src[:, None, :]
    first_same = jnp.min(jnp.where(same, eight[None, None, :], 8), axis=2)
    is_first = cross & (first_same == eight[None, :])
    before = (eight[None, :] < eight[:, None]).astype(jnp.int32)
    rank = jnp.sum(is_first[:, None, :].astype(jnp.int32) * before[None], axis=2)
    slot = jnp.sum(jnp.where(first_same[:, :, None] == eight, rank[:, None, :], 0), axis=2)
    count = jnp.max(jnp.sum(is_first.astype(jnp.int32), axis=1))
    holds = is_first[:, :, None] & (rank[:, :, None] == eight)
    slot_src = jnp.sum(jnp.where(holds, src[:, :, None], 0), axis=1)
    return src, cross.astype(jnp.int32), slot, slot_src, count


def store_kernel(*refs):
    back_ref, outs = refs[0], refs[-3:]
    cc = back_ref.shape[3]
    for g in range(2):
        for k in range(3):
            outs[k][:, g * cc : (g + 1) * cc] = back_ref[g, k]


def store(outs, back, chunk):
    part, cc = back.shape[2:]
    out_spec = pl.BlockSpec((part, 2 * cc), lambda q: (q, chunk))
    return pl.pallas_call(
        store_kernel,
        grid=(4,),
        in_specs=[pl.BlockSpec((2, 3, part, cc), lambda q: (q, 0, 0, 0))] + [ANYWHERE] * len(outs),
        out_specs=[out_spec] * 3,
        out_shape=[jax.ShapeDtypeStruct((4 * part, 2 * cc * CHUNKS), BF16)] * 3,
        input_output_aliases={1 + k: k for k in range(len(outs))},
        compiler_params=STORE_PARAMS,
        cost_estimate=SMALL,
        name="store",
    )(back, *outs)


def gather_rows(w_ref, own_ref, other_ref):
    rows = own_ref.shape[0]

    @pl.when(pl.program_id(0) == 0)
    def _():
        w_ref[:rows] = own_ref[...]
        w_ref[rows:] = other_ref[...]


def input_grad_kernel(y_ref, *refs):
    *ins, w_ref = refs
    cots, (own_ref, other_ref, x_ref), outs, gain_ref = ins[:-8], ins[-8:-5], ins[-5:-1], ins[-1]
    gather_rows(w_ref, own_ref, other_ref)
    turn = pl.program_id(0)
    total = None
    cut = cots[0].shape[1]
    for i, cot in enumerate(cots):
        term = lax.dot_general(
            cot[...],
            w_ref[:, i * cut : (i + 1) * cut],
            (((1,), (1,)), ((), ())),
            preferred_element_type=F32,
        )
        total = term if total is None else total + term

    for d in range(4):

        @pl.when(turn == d)
        def _():
            outs[d][...] = total.astype(BF16)

    @pl.when(turn == 0)
    def _():
        gain_ref[...] = jnp.zeros_like(gain_ref)

    gain_ref[...] += jnp.sum(total * x_ref[...].astype(F32), axis=0, keepdims=True)


def input_grads(cots, w, x, y):
    count, depth = x.shape
    step = count // 4
    row = lambda i, y_ref: ((y_ref[0] + i) % 4, 0)
    whole = lambda i, y_ref: (0, 0)
    *grads, gain = pl.pallas_call(
        input_grad_kernel,
        grid_spec=pltpu.PrefetchScalarGridSpec(
            num_scalar_prefetch=1,
            grid=(4,),
            in_specs=[pl.BlockSpec((step, c.shape[1]), row) for c in cots]
            + [pl.BlockSpec(half.shape, whole) for half in w]
            + [pl.BlockSpec((step, depth), row)],
            out_specs=[pl.BlockSpec((step, depth), whole)] * 4 + [pl.BlockSpec((1, depth), whole)],
            scratch_shapes=[pltpu.VMEM((depth, w[0].shape[1]), BF16)],
        ),
        out_shape=[jax.ShapeDtypeStruct((step, depth), BF16)] * 4
        + [jax.ShapeDtypeStruct((1, depth), F32)],
        compiler_params=PARAMS,
        cost_estimate=SMALL,
        name="input_grads",
    )(y[None], *cots, *w, x)
    return grads, gain


def value_kernel(y_ref, x_ref, w_own_ref, w_other_ref, *refs):
    *outs, w_ref = refs
    gather_rows(w_ref, w_own_ref, w_other_ref)
    turn = pl.program_id(0)
    part = jnp.dot(x_ref[...], w_ref[...], preferred_element_type=F32).astype(BF16)
    half = part.shape[1] // 2
    for d, out in ((0, outs[0]), (1, outs[1]), (3, outs[4])):

        @pl.when(turn == d)
        def _():
            out[...] = part

    @pl.when(turn == 2)
    def _():
        outs[2][...] = part[:, :half]
        outs[3][...] = part[:, half:]


def value_parts(x, w, y):
    count, depth = x.shape
    width = w[0].shape[1]
    step = count // 4
    whole = lambda i, y_ref: (0, 0)
    widths = [width, width, width // 2, width // 2, width]
    return pl.pallas_call(
        value_kernel,
        grid_spec=pltpu.PrefetchScalarGridSpec(
            num_scalar_prefetch=1,
            grid=(4,),
            in_specs=[pl.BlockSpec((step, depth), lambda i, y_ref: ((y_ref[0] + i) % 4, 0))]
            + [pl.BlockSpec(half.shape, whole) for half in w],
            out_specs=[pl.BlockSpec((step, n), whole) for n in widths],
            scratch_shapes=[pltpu.VMEM((depth, width), BF16)],
        ),
        out_shape=[jax.ShapeDtypeStruct((step, n), BF16) for n in widths],
        compiler_params=PARAMS,
        cost_estimate=SMALL,
        name="value_parts",
    )(y[None], x, *w)


def last_used(index, used):
    order = jnp.arange(index.shape[0], dtype=jnp.int32)
    seen = used[None, :] & (order[None, :] <= order[:, None])
    at = jnp.maximum(jnp.max(jnp.where(seen, order[None, :], -1), axis=1), 0)
    return jnp.sum(jnp.where(at[:, None] == order[None, :], index[None, :], 0), axis=1)


def shards(
    hidden,
    value_grad,
    weight,
    moment_one,
    moment_two,
    norm_gain,
    gain_first,
    gain_second,
    donors,
    recipient,
):
    member = lax.axis_index("member")
    fsdp = lax.axis_index("fsdp")
    z, xl, core = member // 4, (member // 2) % 2, member % 2
    xh, y = fsdp // 4, fsdp % 4
    y_at = [(y + d) % 4 for d in range(4)]
    y_from = [(y - d) % 4 for d in range(4)]

    tokens, features = hidden.shape[1:]
    width = value_grad.shape[2]
    rows = features // 8
    cut = width // CHUNKS

    source = jnp.where(recipient == 1, donors, jnp.arange(16, dtype=jnp.int32))
    src, cross, slot, slot_src, count = crossing(source)
    place = lambda s: s // 4 * 2 + s % 2
    my_src, my_cross, my_slot = pick(src, xl), pick(cross, xl), pick(slot, xl)
    leaving = place(pick(slot_src, 1 - xl))
    near_place = last_used(place(my_src), my_cross == 0)
    far_slot = last_used(my_slot, my_cross == 1)
    table = jnp.stack([my_cross, near_place, far_slot])
    table_few = jnp.stack([my_cross, near_place, jnp.minimum(far_slot, SLOTS - 1)])

    blocks = split_inputs(hidden[0], norm_gain, xh)
    pieces = [pick(blocks, y_at[d]) for d in (1, 2, 3)]
    arrived = [to_fsdp(piece, dy=d) for d, piece in zip((1, 2, 3), pieces)]
    w_quarter = [weight[0], to_fsdp(weight[0], dx=1)]

    cots = [
        lax.all_gather(
            value_grad[0, :, i * cut : (i + 1) * cut], "fsdp", axis_index_groups=Y_GROUPS, tiled=True
        )
        for i in range(CHUNKS)
    ]

    spread = spread_states([tie(weight[0], pieces), moment_one[0], moment_two[0]])
    held0 = swap_members(spread[0])
    sent = take_pieces(held0, leaving[:SLOTS])
    far_held0 = to_member(sent, dx=1)
    arrived, blocks, w_quarter, _ = lax.optimization_barrier((arrived, blocks, w_quarter, sent))
    inputs = put_blocks(blocks, arrived, jnp.stack(y_from[1:])).reshape(4 * tokens, 2 * rows)

    partial0 = matmul(inputs, cots[0], (0, 0)).astype(BF16)
    held1 = swap_members(tie(spread[1], partial0, far_held0))

    value_part = value_parts(tie(inputs, partial0), w_quarter, y)

    came0 = tie(to_fsdp(partial0[rows:], dx=1), far_held0, value_part[0])
    sum0 = add_halves(partial0, came0)
    cots[1] = tie(cots[1], sum0)
    partial1 = matmul(inputs, cots[1], (0, 0)).astype(BF16)

    def many(near, far):
        rest = leaving[SLOTS:]
        more = [to_member(take_pieces(pool, rest), dx=1) for pool in near]
        far = [jnp.concatenate(pair) for pair in zip(far, more)]
        return adam_of_sources(table, near, far)

    def new_states(near, far):
        return lax.cond(
            count > SLOTS, many, lambda near, far: adam_of_sources(table_few, near, far), near, far
        )

    grad0 = swap_members(tie(sum0, held1, partial1))
    sent = take_pieces(grad0, leaving[:SLOTS])
    far_grad0 = to_member(sent, dx=1)

    input_grad, gain_part = input_grads(cots, w_quarter, tie(inputs, partial1), y)
    value_got = {1: to_fsdp(value_part[1], dy=1), 3: to_fsdp(value_part[4], dy=3)}
    value_got[2] = [to_fsdp(half, dy=2) for half in value_part[2:4]]

    came1 = to_fsdp(partial1[rows:], dx=1)
    came1 = tie(came1, input_grad[0], sent, value_got[1], value_got[3])
    sum1 = add_halves(partial1, came1)
    new0 = new_states([held0, grad0], [far_held0, tie(far_grad0, sum1)])
    grad1 = tie(swap_members(sum1), new0)
    far_held1 = to_member(take_pieces(tie(held1, new0), leaving[:SLOTS]), dx=1)
    back0 = swap_members(tie(new0, grad1, value_got[2][0]))
    sent = take_pieces(grad1, leaving[:SLOTS])
    far_grad1 = to_member(tie(sent, far_held1), dx=1)
    new1 = new_states([held1, grad1], [far_held1, tie(far_grad1, value_got[2][1])])
    back1 = swap_members(new1)

    gain_part = tie(gain_part, sent).reshape(2, rows)
    gain_parts = jnp.zeros((4, 2, rows), F32)
    for d in range(4):
        got = to_fsdp(gain_part, dy=d) if d else gain_part
        gain_parts = put(gain_parts, got, y_from[d])
    grads_got = [to_fsdp(tie(input_grad[d], far_grad1), dy=d) for d in (1, 2, 3)]
    gain_sum = gain_parts + to_fsdp(gain_parts, dx=1)[:, ::-1]
    gain_sum = jnp.where(xh == 0, gain_sum, gain_sum[:, ::-1]).transpose(1, 0, 2)
    gain_grad = gain_sum.reshape(1, features) / (1.0 + norm_gain)
    gain_new = jnp.concatenate(
        adam_update(norm_gain, gain_grad, gain_first, gain_second, 0.0)
    )
    gain_every = lax.all_gather(jnp.pad(gain_new, ((0, 2), (0, 0))), "member")
    gain_all = pick(gain_every, pick(source, member))[:3, None]

    outs = store(store([], back0, 0), back1, 1)

    parts = [input_grad[0]] + grads_got
    value_parts_got = [value_part[0], value_got[1], value_got[3], *value_got[2]]
    hidden_grad, values = join_parts(
        hidden[0], tie(norm_gain, new1), parts, value_parts_got, xh, y
    )
    return (
        values[None],
        hidden_grad[None],
        *(out[None] for out in outs),
        gain_all[0],
        gain_all[1],
        gain_all[2],
    )


def solution(mesh):
    tok = P("member", "fsdp", None)
    mem = P("member", None)
    return jax.shard_map(
        shards,
        mesh=mesh,
        in_specs=(tok,) * 5 + (mem,) * 3 + (P(), P()),
        out_specs=(tok,) * 5 + (mem,) * 3,
        check_vma=False,
    )
```
